32 devices in a mesh: cfg: 2 (over core), seq: 4 (over z), blk: 4 (over y, x).
Axes of the slice: x: 2, y: 2, z: 4, core: 2. Of those that a mesh axis runs over, the one named last changes fastest.
Arguments:
- img_hidden: bfloat16 [2, 2, 2048, 1536], P('cfg', None, 'seq', 'blk'), may hold values from -15 to 15
- txt_hidden: bfloat16 [2, 2, 160, 1536], P('cfg', None, 'seq', 'blk'), may hold values from -6 to 6
- img_mod: float32 [2, 2, 6, 1536], P('cfg'), may hold values from -9 to 9
- txt_mod: float32 [2, 2, 2, 1536], P('cfg'), may hold values from -3 to 3
- out_mod: float32 [2, 2, 2, 1536], P('cfg'), may hold values from -3 to 3
- w_qkv: bfloat16 [3, 1536, 1536], P(None, None, 'blk'), may hold values from -0.25 to 0.25
- w_txt_kv: bfloat16 [2, 1536, 1536], P(None, None, 'blk'), may hold values from -0.25 to 0.25
- w_out: bfloat16 [1536, 1536], P('blk'), may hold values from -0.15625 to 0.15625
- w_fc1: bfloat16 [1536, 6144], P(None, 'blk'), may hold values from -0.15625 to 0.15625
- w_fc2: bfloat16 [6144, 1536], P('blk'), may hold values from -0.078125 to 0.078125
- w_proj: bfloat16 [1536, 64], P('blk'), may hold values from -0.15625 to 0.15625
- latent: float32 [2, 2048, 64], P(None, 'seq', 'cfg'), may hold values from -6 to 6
- lengths: int32 [2, 2], P('cfg'), may hold values from 1 to 154, as said below
- t_index: int32 [2], replicated, may hold values from 0 to 24
- stride: int32 [2], replicated, may hold values from 1 to 4
- guide: float32 [2], replicated, may hold values from 4 to 8
Outputs:
- new_latent: float32 [2, 2048, 64], P(None, 'seq', 'cfg')
- update_max: float32 [2], replicated
The draws below stay inside these ranges and needn't reach their ends.
Inputs may be any that keep to these rules, and one draw needn't show every extreme that they name: `lengths`: at least one entry equals 154.
All inputs are finite; a program needn't handle non-finite values.
Results may differ from the reference program's by a relative error of at most 0.015.
Values may be sent and summed in bfloat16 or wider, within the bound.
A program may use at most 192 MiB of HBM per device.

```python
import jax
import jax.numpy as jnp
from jax import lax

D = 1536
HEADS = 24
HEAD = 64
FF = 6144
OUT_CH = 64
PROMPTS = 2
TXT = 160
TXT_MAX = 154
STEPS = 28
IMG = 2048


def draw_lengths(key, part):
    first_key, second_key = jax.random.split(key)
    entries = 2 * PROMPTS
    drawn = jax.random.randint(first_key, (entries,), 1, TXT_MAX + 1, dtype=jnp.int32)
    chosen = jax.random.randint(second_key, (), 0, entries, dtype=jnp.int32)
    drawn = jnp.where(jnp.arange(entries, dtype=jnp.int32) == chosen, TXT_MAX, drawn)
    return drawn.reshape(2, PROMPTS)


def draw_img_mod(key, part):
    row_scale = jnp.array([0.5, 0.5, 1.0, 0.5, 0.5, 1.0], dtype=jnp.float32)[None, None, :, None]
    full_shape = (2, PROMPTS, 6, D)
    noise_key = jax.random.fold_in(jax.random.fold_in(key, 11), 0)
    base = jnp.clip(jax.random.normal(noise_key, full_shape, jnp.float32), -4.0, 4.0)
    return base * row_scale


def draw_img_hidden(key, part):
    full_shape = (2, PROMPTS, IMG, D)
    noise_key = jax.random.fold_in(key, 23)
    position = jnp.arange(D, dtype=jnp.float32) / (D - 1)
    feature_scale = 0.4 * jnp.exp(position * jnp.log(6.0))
    base = jnp.clip(jax.random.normal(noise_key, full_shape, jnp.float32), -6.0, 6.0)
    return (base * feature_scale).astype(jnp.bfloat16)


def shard_levels(rng, shape, cuts, smallest, top_value):
    level = 1.0
    for axis_at, shards_of in cuts:
        draws = jax.random.uniform(jax.random.fold_in(jax.random.fold_in(rng, 6), axis_at), (shards_of,), jnp.float32, smallest / len(cuts), top_value / len(cuts))
        level = level * jnp.repeat(jnp.exp(draws), shape[axis_at] // shards_of).reshape((-1,) + (1,) * (len(shape) - 1 - axis_at))
    return level


def gaussian(stream_key, extent, scale, limit, cuts=(), held_as=jnp.bfloat16):
    values = scale * jax.random.normal(stream_key, extent, jnp.float32)
    if cuts:
        values = values * shard_levels(stream_key, extent, cuts, -0.22, 0.18)
    return jnp.clip(values, -limit, limit).astype(held_as)


def setup_inputs(seed: int = 0) -> dict:
    key_list = jax.random.split(jax.random.key(seed), 17)
    return {
        "img_hidden": draw_img_hidden(jax.random.fold_in(key_list[16], 71), 0),
        "txt_hidden": gaussian(key_list[1], (2, PROMPTS, TXT, D), 1.0, 6.0, ((0, 2), (2, 4), (3, 4))),
        "img_mod": draw_img_mod(jax.random.fold_in(key_list[16], 71), 0),
        "txt_mod": gaussian(key_list[3], (2, PROMPTS, 2, D), 0.5, 3.0, ((0, 2),), jnp.float32),
        "out_mod": gaussian(key_list[4], (2, PROMPTS, 2, D), 0.5, 3.0, ((0, 2),), jnp.float32),
        "w_qkv": gaussian(key_list[5], (3, D, D), (D // 3) ** -0.5, 0.25, ((2, 4),)),
        "w_txt_kv": gaussian(key_list[6], (2, D, D), (D // 3) ** -0.5, 0.25, ((2, 4),)),
        "w_out": gaussian(key_list[7], (D, D), D ** -0.5, 0.15625, ((0, 4),)),
        "w_fc1": gaussian(key_list[8], (D, FF), D ** -0.5, 0.15625, ((1, 4),)),
        "w_fc2": gaussian(key_list[9], (FF, D), FF ** -0.5, 0.078125, ((0, 4),)),
        "w_proj": gaussian(key_list[10], (D, OUT_CH), D ** -0.5, 0.15625, ((0, 4),)),
        "latent": gaussian(key_list[11], (PROMPTS, IMG, OUT_CH), 1.0, 6.0, ((1, 4), (2, 2)), jnp.float32),
        "lengths": draw_lengths(jax.random.fold_in(key_list[16], 71), 0),
        "t_index": jax.random.randint(key_list[13], (PROMPTS,), 0, STEPS - 3).astype(jnp.int32),
        "stride": jax.random.randint(key_list[14], (PROMPTS,), 1, 5).astype(jnp.int32),
        "guide": jnp.clip(jax.random.uniform(key_list[15], (PROMPTS,), jnp.float32, 4.0, 8.0), 4.0, 8.0),
    }


EPSILON = 1e-06

def normalize(values):
    values = values.astype(jnp.float32)
    center = lax.optimization_barrier(jnp.mean(values, axis=-1, keepdims=True))
    spread = lax.optimization_barrier(jnp.mean(jnp.square(values - center), axis=-1, keepdims=True))
    return (values - center) * lax.rsqrt(spread + EPSILON)

def modulate(values, scale_row, shift_row):
    return (normalize(values) * (1.0 + scale_row[:, None, :]) + shift_row[:, None, :]).astype(jnp.bfloat16)

def project(values, weight):
    flat_rows = values.reshape(-1, values.shape[-1])
    result = jnp.dot(flat_rows, weight, preferred_element_type=jnp.float32)
    return result.reshape(values.shape[:-1] + (weight.shape[-1],))

def noise_level(step_index):
    remain = 1.0 - step_index.astype(jnp.float32) / STEPS
    return 3.0 * remain / (1.0 + 2.0 * remain)

def one_half(image_in, text_in, image_mod, text_mod, final_mod, text_limit, w_qkv, w_txt_kv, w_out, w_fc1, w_fc2, w_proj):
    attn_in = modulate(image_in, image_mod[:, 1], image_mod[:, 0])
    queries = project(attn_in, w_qkv[0]).astype(jnp.bfloat16)
    keys_img = project(attn_in, w_qkv[1]).astype(jnp.bfloat16)
    values_img = project(attn_in, w_qkv[2]).astype(jnp.bfloat16)
    text_norm = modulate(text_in, text_mod[:, 0], text_mod[:, 1])
    text_keys = project(text_norm, w_txt_kv[0]).astype(jnp.bfloat16)
    text_values = project(text_norm, w_txt_kv[1]).astype(jnp.bfloat16)
    key_rows = jnp.concatenate([keys_img, text_keys], axis=1)
    value_rows = jnp.concatenate([values_img, text_values], axis=1)
    position = jnp.arange(TXT, dtype=jnp.int32)
    live_mask = jnp.concatenate([jnp.ones((PROMPTS, IMG), dtype=bool), position[None, :] < text_limit[:, None]], axis=1)
    head_queries = queries.reshape(PROMPTS, IMG, HEADS, HEAD).transpose(2, 0, 1, 3)
    head_keys = key_rows.reshape(PROMPTS, IMG + TXT, HEADS, HEAD).transpose(2, 0, 1, 3)
    head_values = value_rows.reshape(PROMPTS, IMG + TXT, HEADS, HEAD).transpose(2, 0, 1, 3)

    def attend(operands):
        query_h, key_h, value_h = operands
        scores = jnp.einsum('pqe,pke->pqk', query_h.astype(jnp.float32), key_h.astype(jnp.float32)) * HEAD ** (-0.5)
        scores = jnp.where(live_mask[:, None, :], scores, -jnp.inf)
        peak_value = lax.optimization_barrier(jnp.max(scores, axis=-1, keepdims=True))
        weights = jnp.exp(scores - peak_value)
        total_sum = lax.optimization_barrier(jnp.sum(weights, axis=-1, keepdims=True))
        probs = weights.astype(jnp.bfloat16)
        mixed_values = jnp.einsum('pqk,pke->pqe', probs.astype(jnp.float32), value_h.astype(jnp.float32))
        return (mixed_values / total_sum).astype(jnp.bfloat16)
    attended = lax.map(attend, (head_queries, head_keys, head_values))
    attended = attended.transpose(1, 2, 0, 3).reshape(PROMPTS, IMG, D)
    resid_one = (image_in.astype(jnp.float32) + image_mod[:, 2][:, None, :] * project(attended, w_out)).astype(jnp.bfloat16)
    mlp_in = modulate(resid_one, image_mod[:, 4], image_mod[:, 3])
    hidden_units = jax.nn.gelu(project(mlp_in, w_fc1), approximate=True).astype(jnp.bfloat16)
    resid_two = (resid_one.astype(jnp.float32) + image_mod[:, 5][:, None, :] * project(hidden_units, w_fc2)).astype(jnp.bfloat16)
    final_in = modulate(resid_two, final_mod[:, 0], final_mod[:, 1])
    return project(final_in, w_proj)

def reference(img_hidden, txt_hidden, img_mod, txt_mod, out_mod, w_qkv, w_txt_kv, w_out, w_fc1, w_fc2, w_proj, latent, lengths, t_index, stride, guide):
    velocity_cond = one_half(img_hidden[0], txt_hidden[0], img_mod[0], txt_mod[0], out_mod[0], lengths[0], w_qkv, w_txt_kv, w_out, w_fc1, w_fc2, w_proj)
    velocity_uncond = one_half(img_hidden[1], txt_hidden[1], img_mod[1], txt_mod[1], out_mod[1], lengths[1], w_qkv, w_txt_kv, w_out, w_fc1, w_fc2, w_proj)
    guided = velocity_uncond + guide[:, None, None] * (velocity_cond - velocity_uncond)
    step_size = noise_level(t_index + stride) - noise_level(t_index)
    update = step_size[:, None, None] * guided
    new_latent = latent + update
    update_max = lax.optimization_barrier(jnp.max(jnp.abs(update), axis=(1, 2)))
    return (new_latent, update_max)
```

```python
import functools

import jax
import jax.numpy as jnp
from jax import lax
from jax.experimental import pallas as pl
from jax.experimental.pallas import tpu as pltpu
from jax.sharding import PartitionSpec as P

HEAD = 64
STEPS = 28
EPSILON = 1e-06
PAIR = 2 * HEAD
Q_ROWS = 256
TEXT_PAD = 256


def normalize(values):
    values = values.astype(jnp.float32)
    center = jnp.mean(values, axis=-1, keepdims=True)
    spread = jnp.mean(jnp.square(values - center), axis=-1, keepdims=True)
    return (values - center) * lax.rsqrt(spread + EPSILON)


def modulate(values, scale_row, shift_row):
    return (normalize(values) * (1.0 + scale_row) + shift_row).astype(jnp.bfloat16)


def dot(a, b):
    return jnp.dot(a, b, preferred_element_type=jnp.float32)


def noise_level(step_index):
    remain = 1.0 - step_index.astype(jnp.float32) / STEPS
    return 3.0 * remain / (1.0 + 2.0 * remain)


def attend_kernel(first, last, *refs):
    refs = list(refs)
    q_ref, k_ref, v_ref = refs[:3]
    refs = refs[3:]
    if not first:
        acc_in, top_in = refs[:2]
        refs = refs[2:]
    if last:
        limit_ref, tk_ref, tv_ref = refs[:3]
        refs = refs[3:]
    q = q_ref[...]
    lane = lax.broadcasted_iota(jnp.int32, (1, PAIR), 1)
    scale = HEAD ** (-0.5)
    results = []
    for h in range(2):
        own = (lane < HEAD) if h == 0 else (lane >= HEAD)
        qh = jnp.where(own, q, jnp.zeros_like(q))
        pieces = [(k_ref[...], v_ref[...], None)]
        if last:
            slot = lax.broadcasted_iota(jnp.int32, (1, tk_ref.shape[0]), 1)
            pieces.append((tk_ref[...], tv_ref[...], slot < limit_ref[0]))
        scores = []
        top = None if first else top_in[h]
        for k, v, live in pieces:
            s = lax.dot_general(qh, k, (((1,), (1,)), ((), ())), preferred_element_type=jnp.float32)
            if live is not None:
                s = jnp.where(live, s, -jnp.inf)
            scores.append(s)
            peak = jnp.max(s, axis=-1, keepdims=True)
            if top is None:
                top = jnp.broadcast_to(peak, (q.shape[0], PAIR))
            else:
                top = jnp.maximum(top, peak)
        acc = None if first else acc_in[h] * jnp.exp((top_in[h] - top) * scale)
        for (k, v, live), s in zip(pieces, scores):
            p = jnp.exp((s - top[:, :1]) * scale).astype(jnp.bfloat16)
            vh = jnp.where(own, v, jnp.ones_like(v))
            part = dot(p, vh)
            acc = part if acc is None else acc + part
        results.append((acc, top))
    if last:
        (out_ref,) = refs
        outs = [acc / pltpu.roll(acc, HEAD, 1) for acc, _ in results]
        out_ref[...] = jnp.where(lane < HEAD, outs[0], outs[1]).astype(jnp.bfloat16)
    else:
        acc_out, top_out = refs
        for h in range(2):
            acc_out[h] = results[h][0]
            top_out[h] = results[h][1]


def attend_piece(queries, keys, values, state, text):
    rows, width = queries.shape
    count = keys.shape[0]
    pairs = width // PAIR
    first, last = state is None, text is not None
    q_spec = pl.BlockSpec((Q_ROWS, PAIR), lambda h, i: (i, h))
    kv_spec = pl.BlockSpec((count, PAIR), lambda h, i: (0, h))
    s_spec = pl.BlockSpec((2, Q_ROWS, PAIR), lambda h, i: (h, i, 0))
    args, specs = [queries, keys, values], [q_spec, kv_spec, kv_spec]
    if not first:
        args += list(state)
        specs += [s_spec, s_spec]
    if last:
        args += list(text)
        t_spec = pl.BlockSpec((text[1].shape[0], PAIR), lambda h, i: (0, h))
        specs += [pl.BlockSpec(memory_space=pltpu.SMEM), t_spec, t_spec]
        out_shape = jax.ShapeDtypeStruct((rows, width), jnp.bfloat16)
        out_specs = q_spec
    else:
        out_shape = [jax.ShapeDtypeStruct((2 * pairs, rows, PAIR), jnp.float32)] * 2
        out_specs = [s_spec, s_spec]
    return pl.pallas_call(
        functools.partial(attend_kernel, first, last),
        grid=(pairs, rows // Q_ROWS),
        in_specs=specs,
        out_specs=out_specs,
        out_shape=out_shape,
        compiler_params=pltpu.CompilerParams(vmem_limit_bytes=40 * 1024 * 1024),
        cost_estimate=pl.CostEstimate(
            flops=8 * rows * count * width,
            bytes_accessed=8 * rows * width,
            transcendentals=rows * count * width // HEAD,
        ),
    )(*args)


def per_device(
    img_hidden, txt_hidden, img_mod, txt_mod, out_mod, w_qkv, w_txt_kv, w_out,
    w_fc1, w_fc2, w_proj, latent, lengths, t_index, stride, guide,
):
    seq_size, blk_size = lax.axis_size("seq"), lax.axis_size("blk")
    group = seq_size // 2
    seq_at, blk_at, half = lax.axis_index("seq"), lax.axis_index("blk"), lax.axis_index("cfg")
    prompt = seq_at // group
    img_rows = img_hidden.shape[2]
    rows = 2 * img_rows
    own_rows = rows // blk_size

    def pick(values):
        return lax.dynamic_index_in_dim(values, prompt, 0, keepdims=False)

    def other(values):
        return lax.dynamic_index_in_dim(values, 1 - prompt, 0, keepdims=False)

    swap = [(i, (i + group) % seq_size) for i in range(seq_size)]
    swapped = lax.ppermute(other(img_hidden[0]), "seq", swap)
    mine = jnp.concatenate([pick(img_hidden[0]), swapped], axis=0)
    image = lax.all_gather(mine, "blk", axis=1, tiled=True)
    text = lax.all_gather(txt_hidden[0], "blk", axis=2, tiled=True)
    text = lax.all_gather(text, "seq", axis=1, tiled=True)
    text = pick(text)

    mod = pick(img_mod[0])
    tmod = pick(txt_mod[0])
    fmod = pick(out_mod[0])
    attn_in = modulate(image, mod[1:2], mod[0:1])
    keys = dot(attn_in, w_qkv[1]).astype(jnp.bfloat16)
    values = dot(attn_in, w_qkv[2]).astype(jnp.bfloat16)
    pieces = [(keys, values)]
    for k in range(1, group):
        turn = [
            (i, (i // group) * group + (i + k) % group) for i in range(seq_size)
        ]
        pieces.append((lax.ppermute(keys, "seq", turn), lax.ppermute(values, "seq", turn)))
    queries = dot(attn_in, w_qkv[0]).astype(jnp.bfloat16)
    text_norm = modulate(text, tmod[0:1], tmod[1:2])
    slots = text.shape[0]
    text_norm = jnp.pad(text_norm, ((0, -slots % TEXT_PAD), (0, 0)))
    text_keys = dot(text_norm, w_txt_kv[0]).astype(jnp.bfloat16)
    text_values = dot(text_norm, w_txt_kv[1]).astype(jnp.bfloat16)
    limit = pick(lengths[0])[None]

    full_out = lax.all_gather(w_out, "blk", axis=0, tiled=True)
    full_proj = lax.all_gather(w_proj, "blk", axis=0, tiled=True)

    state = None
    for at, (k, v) in enumerate(pieces):
        tail = (limit, text_keys, text_values) if at == len(pieces) - 1 else None
        state = attend_piece(queries, k, v, state, tail)
    attended = lax.all_gather(state, "blk", axis=1, tiled=True)
    resid_one = (image.astype(jnp.float32) + mod[2:3] * dot(attended, full_out)).astype(
        jnp.bfloat16
    )
    mlp_in = modulate(resid_one, mod[4:5], mod[3:4])
    hidden_units = jax.nn.gelu(dot(mlp_in, w_fc1), approximate=True).astype(jnp.bfloat16)
    mlp_sum = lax.psum_scatter(
        dot(hidden_units, w_fc2).astype(jnp.bfloat16), "blk", scatter_dimension=0, tiled=True
    ).astype(jnp.float32)
    resid_own = lax.dynamic_slice_in_dim(resid_one, blk_at * own_rows, own_rows, 0)
    resid_two = (resid_own.astype(jnp.float32) + mod[5:6] * mlp_sum).astype(jnp.bfloat16)
    final_in = modulate(resid_two, fmod[0:1], fmod[1:2])
    velocity = dot(final_in, full_proj).astype(jnp.bfloat16)

    velocity = lax.all_gather(velocity, "blk", axis=0, tiled=True)
    back = lax.ppermute(velocity[img_rows:], "seq", swap)
    here = velocity[:img_rows]
    both = jnp.where(prompt == 0, jnp.stack([here, back]), jnp.stack([back, here]))
    width = latent.shape[2]
    outgoing = lax.dynamic_slice_in_dim(both, (1 - half) * width, width, 2)
    own = lax.dynamic_slice_in_dim(both, half * width, width, 2).astype(jnp.float32)
    arrived = lax.ppermute(outgoing, "cfg", [(0, 1), (1, 0)]).astype(jnp.float32)
    cond = jnp.where(half == 0, own, arrived)
    uncond = jnp.where(half == 0, arrived, own)
    guided = uncond + guide[:, None, None] * (cond - uncond)
    step_size = noise_level(t_index + stride) - noise_level(t_index)
    update = step_size[:, None, None] * guided
    peak = lax.pmax(jnp.max(jnp.abs(update), axis=(1, 2)), ("cfg", "seq"))
    return (latent + update, peak)


def solution(mesh):
    placed = (
        P("cfg", None, "seq", "blk"),
        P("cfg", None, "seq", "blk"),
        P("cfg", None, None, None),
        P("cfg", None, None, None),
        P("cfg", None, None, None),
        P(None, None, "blk"),
        P(None, None, "blk"),
        P("blk", None),
        P(None, "blk"),
        P("blk", None),
        P("blk", None),
        P(None, "seq", "cfg"),
        P("cfg", None),
        P(),
        P(),
        P(),
    )
    return jax.shard_map(
        per_device,
        mesh=mesh,
        in_specs=placed,
        out_specs=(P(None, "seq", "cfg"), P()),
        check_vma=False,
    )
```

```python
import functools

import jax
import jax.numpy as jnp
from jax import lax
from jax.experimental import pallas as pl
from jax.experimental.pallas import tpu as pltpu
from jax.sharding import PartitionSpec as P

HEAD = 64
STEPS = 28
EPSILON = 1e-06
PAIR = 2 * HEAD
Q_ROWS = 256
TEXT_PAD = 256


def normalize(values):
    values = values.astype(jnp.float32)
    center = jnp.mean(values, axis=-1, keepdims=True)
    spread = jnp.mean(jnp.square(values - center), axis=-1, keepdims=True)
    return (values - center) * lax.rsqrt(spread + EPSILON)


def modulate(values, scale_row, shift_row):
    return (normalize(values) * (1.0 + scale_row) + shift_row).astype(jnp.bfloat16)


def dot(a, b):
    return jnp.dot(a, b, preferred_element_type=jnp.float32)


def noise_level(step_index):
    remain = 1.0 - step_index.astype(jnp.float32) / STEPS
    return 3.0 * remain / (1.0 + 2.0 * remain)


def attend_kernel(first, last, *refs):
    refs = list(refs)
    q_ref, k_ref, v_ref = refs[:3]
    refs = refs[3:]
    if not first:
        acc_in, top_in = refs[:2]
        refs = refs[2:]
    if last:
        live_ref, tk_ref, tv_ref = refs[:3]
        refs = refs[3:]
    q = q_ref[...]
    lane = lax.broadcasted_iota(jnp.int32, (1, PAIR), 1)
    scale = HEAD ** (-0.5)
    results = []
    for h in range(2):
        own = (lane < HEAD) if h == 0 else (lane >= HEAD)
        qh = jnp.where(own, q, jnp.zeros_like(q))
        pieces = [(k_ref[...], v_ref[...], None)]
        if last:
            pieces.append((tk_ref[...], tv_ref[...], live_ref[...] > 0.5))
        scores = []
        top = None if first else top_in[h]
        for k, v, live in pieces:
            s = lax.dot_general(qh, k, (((1,), (1,)), ((), ())), preferred_element_type=jnp.float32)
            if live is not None:
                s = jnp.where(live, s, -jnp.inf)
            scores.append(s)
            peak = jnp.max(s, axis=-1, keepdims=True)
            if top is None:
                top = jnp.broadcast_to(peak, (q.shape[0], PAIR))
            else:
                top = jnp.maximum(top, peak)
        acc = None if first else acc_in[h] * jnp.exp((top_in[h] - top) * scale)
        for (k, v, live), s in zip(pieces, scores):
            p = jnp.exp((s - top[:, :1]) * scale).astype(jnp.bfloat16)
            vh = jnp.where(own, v, jnp.ones_like(v))
            part = dot(p, vh)
            acc = part if acc is None else acc + part
        results.append((acc, top))
    if last:
        (out_ref,) = refs
        outs = [acc / pltpu.roll(acc, HEAD, 1) for acc, _ in results]
        out_ref[...] = jnp.where(lane < HEAD, outs[0], outs[1]).astype(jnp.bfloat16)
    else:
        acc_out, top_out = refs
        for h in range(2):
            acc_out[h] = results[h][0]
            top_out[h] = results[h][1]


def attend_piece(queries, keys, values, state, text):
    rows, width = queries.shape
    count = keys.shape[0]
    pairs = width // PAIR
    first, last = state is None, text is not None
    q_spec = pl.BlockSpec((Q_ROWS, PAIR), lambda h, i: (i, h))
    kv_spec = pl.BlockSpec((count, PAIR), lambda h, i: (0, h))
    s_spec = pl.BlockSpec((2, Q_ROWS, PAIR), lambda h, i: (h, i, 0))
    args, specs = [queries, keys, values], [q_spec, kv_spec, kv_spec]
    if not first:
        args += list(state)
        specs += [s_spec, s_spec]
    if last:
        args += list(text)
        t_spec = pl.BlockSpec((text[1].shape[0], PAIR), lambda h, i: (0, h))
        live_spec = pl.BlockSpec(text[0].shape, lambda h, i: (0, 0))
        specs += [live_spec, t_spec, t_spec]
        out_shape = jax.ShapeDtypeStruct((rows, width), jnp.bfloat16)
        out_specs = q_spec
    else:
        out_shape = [jax.ShapeDtypeStruct((2 * pairs, rows, PAIR), jnp.float32)] * 2
        out_specs = [s_spec, s_spec]
    return pl.pallas_call(
        functools.partial(attend_kernel, first, last),
        grid=(pairs, rows // Q_ROWS),
        in_specs=specs,
        out_specs=out_specs,
        out_shape=out_shape,
        compiler_params=pltpu.CompilerParams(vmem_limit_bytes=40 * 1024 * 1024),
        cost_estimate=pl.CostEstimate(
            flops=8 * rows * count * width,
            bytes_accessed=8 * rows * width,
            transcendentals=rows * count * width // HEAD,
        ),
    )(*args)


MESH = pl.DeviceIdType.MESH
CHUNKS = 4


def remote(src, dst, send, recv, target):
    return pltpu.make_async_remote_copy(
        src_ref=src, dst_ref=dst, send_sem=send, recv_sem=recv,
        device_id=target, device_id_type=MESH,
    )


def gather_kernel(S, B, img, txt, out, tout, s_own, r_own, s_swap, r_swap, s_fwd, r_fwd,
                  s_txt, r_txt, s_tf, r_tf, local):
    s, b, c = lax.axis_index("seq"), lax.axis_index("blk"), lax.axis_index("cfg")
    group = S // 2
    p = s // group
    sp = (s + group) % S
    n, w = img.shape[1:]
    tn = txt.shape[1]
    step = n // CHUNKS
    cols = pl.ds(pl.multiple_of(b * w, w), w)
    barrier = pltpu.get_barrier_semaphore()
    for d in range(1, S):
        pl.semaphore_signal(barrier, inc=1, device_id=(c, (s + d) % S, b), device_id_type=MESH)
    for d in range(1, B):
        pl.semaphore_signal(barrier, inc=1, device_id=(c, s, (b + d) % B), device_id_type=MESH)
    pl.semaphore_wait(barrier, S + B - 2)

    swaps = []
    for j in range(CHUNKS):
        swaps.append(remote(
            img.at[1 - p, pl.ds(j * step, step)], out.at[pl.ds(n + j * step, step), cols],
            s_swap.at[j], r_swap.at[j], (c, sp, b)))
        swaps[-1].start()
    texts = []
    here = pl.ds(pl.multiple_of(s * tn, tn), tn)
    for d in range(1, S):
        t = (s + d) % S
        texts.append(remote(
            txt.at[t // group], tout.at[here, cols], s_txt.at[d - 1], r_txt.at[d - 1], (c, t, b)))
        texts[-1].start()
    own = []
    for d in range(1, B):
        own.append(remote(
            img.at[p], out.at[pl.ds(0, n), cols], s_own.at[d - 1], r_own.at[d - 1],
            (c, s, (b + d) % B)))
        own[-1].start()
    keep = pltpu.make_async_copy(img.at[p], out.at[pl.ds(0, n), cols], local.at[0])
    keep.start()
    keep_text = pltpu.make_async_copy(txt.at[p], tout.at[here, cols], local.at[1])
    keep_text.start()
    keep_text.wait()
    for copy in texts:
        copy.wait()
    spread = []
    for d in range(1, B):
        spread.append(remote(
            tout.at[:, cols], tout.at[:, cols], s_tf.at[d - 1], r_tf.at[d - 1],
            (c, s, (b + d) % B)))
        spread[-1].start()
    for j in range(CHUNKS):
        swaps[j].wait()
        part = out.at[pl.ds(n + j * step, step), cols]
        for d in range(1, B):
            spread.append(remote(
                part, part, s_fwd.at[j, d - 1], r_fwd.at[j, d - 1], (c, s, (b + d) % B)))
            spread[-1].start()
    keep.wait()
    for copy in own + spread:
        copy.wait()


def gather_tokens(img, txt, S, B):
    n, w = img.shape[1:]
    tn = txt.shape[1]
    dma = pltpu.SemaphoreType.DMA
    shapes = [(B - 1,)] * 2 + [(CHUNKS,)] * 2 + [(CHUNKS, B - 1)] * 2 + [(S - 1,)] * 2 + [(B - 1,)] * 2 + [(2,)]
    return pl.pallas_call(
        functools.partial(gather_kernel, S, B),
        out_shape=[
            jax.ShapeDtypeStruct((2 * n, B * w), jnp.bfloat16),
            jax.ShapeDtypeStruct((S * tn, B * w), jnp.bfloat16),
        ],
        in_specs=[pl.BlockSpec(memory_space=pl.ANY)] * 2,
        out_specs=[pl.BlockSpec(memory_space=pl.ANY)] * 2,
        scratch_shapes=[dma(shape) for shape in shapes],
        compiler_params=pltpu.CompilerParams(collective_id=0, has_side_effects=True),
    )(img, txt)


def tail_kernel(S, B, vel, par, out, peak, inbox, box, tops, s_in, r_in, s_box, r_box, s_top, r_top):
    s, b, c = lax.axis_index("seq"), lax.axis_index("blk"), lax.axis_index("cfg")
    group, side = S // 2, B // 2
    p = s // group
    high = b // side
    t = (s + group * high) % S
    me = c * S + s
    barrier = pltpu.get_barrier_semaphore()
    for d in range(1, 2 * S):
        o = (me + d) % (2 * S)
        pl.semaphore_signal(barrier, inc=1, device_id=(o // S, o % S, b), device_id_type=MESH)
    for d in range(1, B):
        pl.semaphore_signal(barrier, inc=1, device_id=(c, s, (b + d) % B), device_id_type=MESH)
    pl.semaphore_wait(barrier, 2 * S - 1 + B - 1)

    across = remote(vel.at[1 - c], inbox.at[c], s_in.at[0], r_in.at[0], (1 - c, t, b))
    across.start()

    @pl.when(high == 0)
    def _():
        inbox[c] = vel[c]

    @pl.when(high == 1)
    def _():
        same = remote(vel.at[c], inbox.at[c], s_in.at[1], r_in.at[1], (c, (s + group) % S, b))
        same.start()
        same.wait()

    across.wait()
    cond = inbox[0].astype(jnp.float32)
    uncond = inbox[1].astype(jnp.float32)
    box[b] = par[1:2] * (uncond + par[0:1] * (cond - uncond))
    sends = []
    for d in range(1, B):
        sends.append(remote(
            box.at[b], box.at[b], s_box.at[d - 1], r_box.at[d - 1], (c, s, (b + d) % B)))
        sends[-1].start()
    for copy in sends:
        copy.wait()
    tall = []
    width = box.shape[2]
    for k in range(2):
        which = p if k == 0 else 1 - p
        top = None
        for j in range(side):
            part = box[k * side + j]
            out[which, :, j * width:(j + 1) * width] = part
            value = jnp.max(jnp.abs(part), axis=(0, 1), keepdims=True)
            top = value if top is None else jnp.maximum(top, value)
        tall.append(top)
    row = lax.broadcasted_iota(jnp.int32, (8, 128), 0)
    tops[me] = jnp.where(row == p, tall[0], tall[1])
    sends = []
    for d in range(1, 2 * S):
        o = (me + d) % (2 * S)
        sends.append(remote(
            tops.at[me], tops.at[me], s_top.at[d - 1], r_top.at[d - 1], (o // S, o % S, b)))
        sends[-1].start()
    for copy in sends:
        copy.wait()
    peak[...] = jnp.max(tops[...], axis=0)


def finish(vel, par, S, B):
    _, chans, width = vel.shape
    dma = pltpu.SemaphoreType.DMA
    vmem = pl.BlockSpec(memory_space=pltpu.VMEM)
    return pl.pallas_call(
        functools.partial(tail_kernel, S, B),
        out_shape=[
            jax.ShapeDtypeStruct((2, chans, width * B // 2), jnp.float32),
            jax.ShapeDtypeStruct((8, 128), jnp.float32),
        ],
        in_specs=[vmem] * 2,
        out_specs=[vmem] * 2,
        scratch_shapes=[
            pltpu.VMEM((2, chans, width), jnp.bfloat16),
            pltpu.VMEM((B, chans, width), jnp.float32),
            pltpu.VMEM((2 * S, 8, 128), jnp.float32),
            dma((2,)), dma((2,)), dma((B - 1,)), dma((B - 1,)),
            dma((2 * S - 1,)), dma((2 * S - 1,)),
        ],
        compiler_params=pltpu.CompilerParams(collective_id=1, has_side_effects=True),
    )(vel, par)


def per_device(
    img_hidden, txt_hidden, img_mod, txt_mod, out_mod, w_qkv, w_txt_kv, w_out,
    w_fc1, w_fc2, w_proj, latent, lengths, t_index, stride, guide,
):
    seq_size, blk_size = lax.axis_size("seq"), lax.axis_size("blk")
    group = seq_size // 2
    seq_at, blk_at, half = lax.axis_index("seq"), lax.axis_index("blk"), lax.axis_index("cfg")
    prompt = seq_at // group
    img_rows = img_hidden.shape[2]
    rows = 2 * img_rows
    own_rows = rows // blk_size

    def pick(values):
        return lax.dynamic_index_in_dim(values, prompt, 0, keepdims=False)

    slots = txt_hidden.shape[2]
    padded = jnp.pad(txt_hidden[0], ((0, 0), (0, -slots % 16), (0, 0)))
    image, text = gather_tokens(img_hidden[0], padded, seq_size, blk_size)

    mod = pick(img_mod[0])
    tmod = pick(txt_mod[0])
    fmod = pick(out_mod[0])
    attn_in = modulate(image, mod[1:2], mod[0:1])
    keys = dot(attn_in, w_qkv[1]).astype(jnp.bfloat16)
    values = dot(attn_in, w_qkv[2]).astype(jnp.bfloat16)
    pieces = [(keys, values)]
    for k in range(1, group):
        turn = [
            (i, (i // group) * group + (i + k) % group) for i in range(seq_size)
        ]
        pieces.append((lax.ppermute(keys, "seq", turn), lax.ppermute(values, "seq", turn)))
    queries = dot(attn_in, w_qkv[0]).astype(jnp.bfloat16)
    text_norm = modulate(text, tmod[0:1], tmod[1:2])
    extra = -text.shape[0] % TEXT_PAD
    text_norm = jnp.pad(text_norm, ((0, extra), (0, 0)))
    text_keys = dot(text_norm, w_txt_kv[0]).astype(jnp.bfloat16)
    text_values = dot(text_norm, w_txt_kv[1]).astype(jnp.bfloat16)
    at = jnp.arange(text_norm.shape[0], dtype=jnp.int32)
    each = padded.shape[1]
    live = (at % each < slots) & (at // each * slots + at % each < pick(lengths[0]))
    live = (live & (at < text.shape[0])).astype(jnp.float32)[None]

    weights = lax.all_gather(
        jnp.concatenate([w_out, w_proj], axis=1), "blk", axis=0, tiled=True
    )
    model_width = w_out.shape[1]
    full_out, full_proj = weights[:, :model_width], weights[:, model_width:]

    state = None
    for at, (k, v) in enumerate(pieces):
        tail = (live, text_keys, text_values) if at == len(pieces) - 1 else None
        state = attend_piece(queries, k, v, state, tail)
    attended = lax.all_gather(state, "blk", axis=1, tiled=True)
    resid_one = (image.astype(jnp.float32) + mod[2:3] * dot(attended, full_out)).astype(
        jnp.bfloat16
    )
    mlp_in = modulate(resid_one, mod[4:5], mod[3:4])
    hidden_units = jax.nn.gelu(dot(mlp_in, w_fc1), approximate=True).astype(jnp.bfloat16)
    mlp_sum = lax.psum_scatter(
        dot(hidden_units, w_fc2).astype(jnp.bfloat16), "blk", scatter_dimension=0, tiled=True
    ).astype(jnp.float32)
    resid_own = lax.dynamic_slice_in_dim(resid_one, blk_at * own_rows, own_rows, 0)
    resid_two = (resid_own.astype(jnp.float32) + mod[5:6] * mlp_sum).astype(jnp.bfloat16)
    final_in = modulate(resid_two, fmod[0:1], fmod[1:2])
    velocity = lax.dot_general(
        full_proj, final_in, (((0,), (1,)), ((), ())), preferred_element_type=jnp.float32
    ).astype(jnp.bfloat16)
    velocity = velocity.reshape(2, velocity.shape[0] // 2, own_rows)
    step_size = noise_level(t_index + stride) - noise_level(t_index)
    chunk_prompt = jnp.where(blk_at < blk_size // 2, prompt, 1 - prompt)
    par = jnp.stack([guide[chunk_prompt], step_size[chunk_prompt]])
    par = jnp.broadcast_to(par[:, None], (2, own_rows))
    update, peak = finish(velocity, par, seq_size, blk_size)
    return (latent + update.transpose(0, 2, 1), peak[:2, 0])


def solution(mesh):
    placed = (
        P("cfg", None, "seq", "blk"),
        P("cfg", None, "seq", "blk"),
        P("cfg", None, None, None),
        P("cfg", None, None, None),
        P("cfg", None, None, None),
        P(None, None, "blk"),
        P(None, None, "blk"),
        P("blk", None),
        P(None, "blk"),
        P("blk", None),
        P("blk", None),
        P(None, "seq", "cfg"),
        P("cfg", None),
        P(),
        P(),
        P(),
    )
    return jax.shard_map(
        per_device,
        mesh=mesh,
        in_specs=placed,
        out_specs=(P(None, "seq", "cfg"), P()),
        check_vma=False,
    )
```

```python
import functools

import jax
import jax.numpy as jnp
from jax import lax
from jax.experimental import pallas as pl
from jax.experimental.pallas import tpu as pltpu
from jax.sharding import PartitionSpec as P

HEAD = 64
STEPS = 28
EPSILON = 1e-06
PAIR = 2 * HEAD
Q_ROWS = 256
TEXT_PAD = 256


def normalize(values):
    values = values.astype(jnp.float32)
    center = jnp.mean(values, axis=-1, keepdims=True)
    spread = jnp.mean(jnp.square(values - center), axis=-1, keepdims=True)
    return (values - center) * lax.rsqrt(spread + EPSILON)


def modulate(values, scale_row, shift_row):
    return (normalize(values) * (1.0 + scale_row) + shift_row).astype(jnp.bfloat16)


def dot(a, b):
    return jnp.dot(a, b, preferred_element_type=jnp.float32)


def noise_level(step_index):
    remain = 1.0 - step_index.astype(jnp.float32) / STEPS
    return 3.0 * remain / (1.0 + 2.0 * remain)


MESH = pl.DeviceIdType.MESH
CHUNKS = 4


def remote(src, dst, send, recv, target):
    return pltpu.make_async_remote_copy(
        src_ref=src, dst_ref=dst, send_sem=send, recv_sem=recv,
        device_id=target, device_id_type=MESH,
    )


def at_ends():
    h, i = pl.program_id(0), pl.program_id(1)
    pairs, blocks = pl.num_programs(0), pl.num_programs(1)
    return h, i, blocks, (h == 0) & (i == 0), (h == pairs - 1) & (i == blocks - 1)


def greet(targets):
    barrier = pltpu.get_barrier_semaphore()
    for target in targets:
        pl.semaphore_signal(barrier, inc=1, device_id=target, device_id_type=MESH)
    pl.semaphore_wait(barrier, len(targets))


def attend_kernel(first, last, S, B, steps, *refs):
    refs = list(refs)
    q_ref, k_ref, v_ref = refs[:3]
    refs = refs[3:]
    if not first:
        acc_in, top_in = refs[:2]
        refs = refs[2:]
    if last:
        live_ref, tk_ref, tv_ref = refs[:3]
        refs = refs[3:]
    s_at, b, c = lax.axis_index("seq"), lax.axis_index("blk"), lax.axis_index("cfg")
    h_at, i_at, blocks, opening, closing = at_ends()
    peers = [(c, s_at, (b + d) % B) for d in range(1, B)]
    if first:
        w_ref, refs = refs[0], refs[1:]
        *refs, s_w, r_w, s_x, r_x, w_sem = refs
        w_full, refs = refs[-1], refs[:-1]
        depth = w_ref.shape[0]
        half = depth // 2

        def share(d):
            rows = pl.ds(pl.multiple_of(b * depth + c * half, half), half)
            return remote(
                w_ref.at[pl.ds(pl.multiple_of(c * half, half), half)], w_full.at[rows],
                s_w.at[d - 1], r_w.at[d - 1], peers[d - 1])

        def cross(d):
            rows = pl.ds(pl.multiple_of((b + B - d) % B * depth + c * half, half), half)
            return remote(
                w_full.at[rows], w_full.at[rows], s_x.at[d - 1], r_x.at[d - 1], (1 - c, s_at, b))

        def keep():
            rows = pl.ds(pl.multiple_of(b * depth, depth), depth)
            return pltpu.make_async_copy(w_ref, w_full.at[rows], w_sem.at[0])

        @pl.when(opening)
        def _():
            greet(peers + [(1 - c, s_at, b)])
            for d in range(1, B):
                share(d).start()
            keep().start()

    if last:
        *refs, held, s_o, r_o, l_o = refs

        def place(at):
            return refs[-1].at[
                pl.ds(pl.multiple_of(at % steps[1] * Q_ROWS, Q_ROWS), Q_ROWS),
                pl.ds(pl.multiple_of(b * (steps[0] * PAIR) + at // steps[1] * PAIR, PAIR), PAIR),
            ]

        def give(at, d):
            return remote(
                held.at[at], place(at), s_o.at[d - 1, at], r_o.at[d - 1, at], peers[d - 1])

        def own_copy(at):
            return pltpu.make_async_copy(held.at[at], place(at), l_o.at[at])

        if not first:
            @pl.when(opening)
            def _():
                greet(peers)

    q = q_ref[...]
    lane = lax.broadcasted_iota(jnp.int32, (1, PAIR), 1)
    scale = HEAD ** (-0.5)
    results = []
    for h in range(2):
        own = (lane < HEAD) if h == 0 else (lane >= HEAD)
        qh = jnp.where(own, q, jnp.zeros_like(q))
        pieces = [(k_ref[...], v_ref[...], None)]
        if last:
            pieces.append((tk_ref[...], tv_ref[...], live_ref[...] > 0.5))
        scores = []
        top = None if first else top_in[h]
        for k, v, live in pieces:
            s = lax.dot_general(qh, k, (((1,), (1,)), ((), ())), preferred_element_type=jnp.float32)
            if live is not None:
                s = jnp.where(live, s, -jnp.inf)
            scores.append(s)
            peak = jnp.max(s, axis=-1, keepdims=True)
            if top is None:
                top = jnp.broadcast_to(peak, (q.shape[0], PAIR))
            else:
                top = jnp.maximum(top, peak)
        acc = None if first else acc_in[h] * jnp.exp((top_in[h] - top) * scale)
        for (k, v, live), s in zip(pieces, scores):
            p = jnp.exp((s - top[:, :1]) * scale).astype(jnp.bfloat16)
            vh = jnp.where(own, v, jnp.ones_like(v))
            part = dot(p, vh)
            acc = part if acc is None else acc + part
        results.append((acc, top))
    if last:
        outs = [acc / pltpu.roll(acc, HEAD, 1) for acc, _ in results]
        now = h_at * steps[1] + i_at
        held[now] = jnp.where(lane < HEAD, outs[0], outs[1]).astype(jnp.bfloat16)
        for d in range(1, B):
            give(now, d).start()
        own_copy(now).start()

        @pl.when(closing)
        def _():
            def drain(at, carry):
                for d in range(1, B):
                    give(at, d).wait()
                own_copy(at).wait()
                return carry

            lax.fori_loop(0, steps[0] * steps[1], drain, 0)
    else:
        acc_out, top_out = refs
        for h in range(2):
            acc_out[h] = results[h][0]
            top_out[h] = results[h][1]
    if first:
        @pl.when(closing)
        def _():
            for d in range(1, B):
                share(d).wait()
                cross(d).start()
            for d in range(1, B):
                cross(d).wait()
            keep().wait()


def attend_piece(queries, keys, values, state, text, weights, S, B):
    rows, width = queries.shape
    count = keys.shape[0]
    pairs = width // PAIR
    steps = (pairs, rows // Q_ROWS)
    total = steps[0] * steps[1]
    dma = pltpu.SemaphoreType.DMA
    first, last = state is None, text is not None
    q_spec = pl.BlockSpec((Q_ROWS, PAIR), lambda h, i: (i, h))
    kv_spec = pl.BlockSpec((count, PAIR), lambda h, i: (0, h))
    s_spec = pl.BlockSpec((2, Q_ROWS, PAIR), lambda h, i: (h, i, 0))
    anywhere = pl.BlockSpec(memory_space=pl.ANY)
    args, specs = [queries, keys, values], [q_spec, kv_spec, kv_spec]
    out_shape, out_specs, scratch = [], [], []
    if not first:
        args += list(state)
        specs += [s_spec, s_spec]
    if last:
        args += list(text)
        t_spec = pl.BlockSpec((text[1].shape[0], PAIR), lambda h, i: (0, h))
        live_spec = pl.BlockSpec(text[0].shape, lambda h, i: (0, 0))
        specs += [live_spec, t_spec, t_spec]
        out_shape += [jax.ShapeDtypeStruct((rows, B * width), jnp.bfloat16)]
        out_specs += [anywhere]
        scratch += [
            pltpu.VMEM((total, Q_ROWS, PAIR), jnp.bfloat16),
            dma((B - 1, total)), dma((B - 1, total)), dma((total,)),
        ]
    else:
        out_shape += [jax.ShapeDtypeStruct((2 * pairs, rows, PAIR), jnp.float32)] * 2
        out_specs += [s_spec, s_spec]
    if first:
        args.append(weights)
        specs.append(anywhere)
        depth, across = weights.shape
        out_shape.append(jax.ShapeDtypeStruct((B * depth, across), jnp.bfloat16))
        out_specs.append(anywhere)
        scratch += [dma((B - 1,))] * 4 + [dma((1,))]
    reach = {"collective_id": 2 if first else 3, "has_side_effects": True} if first or last else {}
    return pl.pallas_call(
        functools.partial(attend_kernel, first, last, S, B, steps),
        grid=steps,
        in_specs=specs,
        out_specs=out_specs,
        out_shape=out_shape,
        scratch_shapes=scratch,
        compiler_params=pltpu.CompilerParams(vmem_limit_bytes=40 * 1024 * 1024, **reach),
        cost_estimate=pl.CostEstimate(
            flops=8 * rows * count * width,
            bytes_accessed=8 * rows * width,
            transcendentals=rows * count * width // HEAD,
        ),
    )(*args)


def gather_kernel(S, B, img, txt, out, tout, s_own, r_own, s_swap, r_swap, s_fwd, r_fwd,
                  s_txt, r_txt, s_tf, r_tf, local):
    s, b, c = lax.axis_index("seq"), lax.axis_index("blk"), lax.axis_index("cfg")
    group = S // 2
    p = s // group
    sp = (s + group) % S
    n, w = img.shape[1:]
    tn = txt.shape[1]
    step = n // CHUNKS
    cols = pl.ds(pl.multiple_of(b * w, w), w)
    barrier = pltpu.get_barrier_semaphore()
    for d in range(1, S):
        pl.semaphore_signal(barrier, inc=1, device_id=(c, (s + d) % S, b), device_id_type=MESH)
    for d in range(1, B):
        pl.semaphore_signal(barrier, inc=1, device_id=(c, s, (b + d) % B), device_id_type=MESH)
    pl.semaphore_wait(barrier, S + B - 2)

    swaps = []
    for j in range(CHUNKS):
        swaps.append(remote(
            img.at[1 - p, pl.ds(j * step, step)], out.at[pl.ds(n + j * step, step), cols],
            s_swap.at[j], r_swap.at[j], (c, sp, b)))
        swaps[-1].start()
    texts = []
    here = pl.ds(pl.multiple_of(s * tn, tn), tn)
    for d in range(1, S):
        t = (s + d) % S
        texts.append(remote(
            txt.at[t // group], tout.at[here, cols], s_txt.at[d - 1], r_txt.at[d - 1], (c, t, b)))
        texts[-1].start()
    own = []
    for d in range(1, B):
        own.append(remote(
            img.at[p], out.at[pl.ds(0, n), cols], s_own.at[d - 1], r_own.at[d - 1],
            (c, s, (b + d) % B)))
        own[-1].start()
    keep = pltpu.make_async_copy(img.at[p], out.at[pl.ds(0, n), cols], local.at[0])
    keep.start()
    keep_text = pltpu.make_async_copy(txt.at[p], tout.at[here, cols], local.at[1])
    keep_text.start()
    keep_text.wait()
    for copy in texts:
        copy.wait()
    spread = []
    for d in range(1, B):
        spread.append(remote(
            tout.at[:, cols], tout.at[:, cols], s_tf.at[d - 1], r_tf.at[d - 1],
            (c, s, (b + d) % B)))
        spread[-1].start()
    for j in range(CHUNKS):
        swaps[j].wait()
        part = out.at[pl.ds(n + j * step, step), cols]
        for d in range(1, B):
            spread.append(remote(
                part, part, s_fwd.at[j, d - 1], r_fwd.at[j, d - 1], (c, s, (b + d) % B)))
            spread[-1].start()
    keep.wait()
    for copy in own + spread:
        copy.wait()


def gather_tokens(img, txt, S, B):
    n, w = img.shape[1:]
    tn = txt.shape[1]
    dma = pltpu.SemaphoreType.DMA
    shapes = [(B - 1,)] * 2 + [(CHUNKS,)] * 2 + [(CHUNKS, B - 1)] * 2 + [(S - 1,)] * 2 + [(B - 1,)] * 2 + [(2,)]
    return pl.pallas_call(
        functools.partial(gather_kernel, S, B),
        out_shape=[
            jax.ShapeDtypeStruct((2 * n, B * w), jnp.bfloat16),
            jax.ShapeDtypeStruct((S * tn, B * w), jnp.bfloat16),
        ],
        in_specs=[pl.BlockSpec(memory_space=pl.ANY)] * 2,
        out_specs=[pl.BlockSpec(memory_space=pl.ANY)] * 2,
        scratch_shapes=[dma(shape) for shape in shapes],
        compiler_params=pltpu.CompilerParams(collective_id=0, has_side_effects=True),
    )(img, txt)


def tail_kernel(S, B, vel, par, out, peak, inbox, box, tops, s_in, r_in, s_box, r_box, s_top, r_top):
    s, b, c = lax.axis_index("seq"), lax.axis_index("blk"), lax.axis_index("cfg")
    group, side = S // 2, B // 2
    p = s // group
    high = b // side
    t = (s + group * high) % S
    me = c * S + s
    barrier = pltpu.get_barrier_semaphore()
    for d in range(1, 2 * S):
        o = (me + d) % (2 * S)
        pl.semaphore_signal(barrier, inc=1, device_id=(o // S, o % S, b), device_id_type=MESH)
    for d in range(1, B):
        pl.semaphore_signal(barrier, inc=1, device_id=(c, s, (b + d) % B), device_id_type=MESH)
    pl.semaphore_wait(barrier, 2 * S - 1 + B - 1)

    across = remote(vel.at[1 - c], inbox.at[c], s_in.at[0], r_in.at[0], (1 - c, t, b))
    across.start()

    @pl.when(high == 0)
    def _():
        inbox[c] = vel[c]

    @pl.when(high == 1)
    def _():
        same = remote(vel.at[c], inbox.at[c], s_in.at[1], r_in.at[1], (c, (s + group) % S, b))
        same.start()
        same.wait()

    across.wait()
    cond = inbox[0].astype(jnp.float32)
    uncond = inbox[1].astype(jnp.float32)
    box[b] = par[1:2] * (uncond + par[0:1] * (cond - uncond))
    sends = []
    for d in range(1, B):
        sends.append(remote(
            box.at[b], box.at[b], s_box.at[d - 1], r_box.at[d - 1], (c, s, (b + d) % B)))
        sends[-1].start()
    for copy in sends:
        copy.wait()
    tall = []
    width = box.shape[2]
    for k in range(2):
        which = p if k == 0 else 1 - p
        top = None
        for j in range(side):
            part = box[k * side + j]
            out[which, :, j * width:(j + 1) * width] = part
            value = jnp.max(jnp.abs(part), axis=(0, 1), keepdims=True)
            top = value if top is None else jnp.maximum(top, value)
        tall.append(top)
    row = lax.broadcasted_iota(jnp.int32, (8, 128), 0)
    tops[me] = jnp.where(row == p, tall[0], tall[1])
    sends = []
    for d in range(1, 2 * S):
        o = (me + d) % (2 * S)
        sends.append(remote(
            tops.at[me], tops.at[me], s_top.at[d - 1], r_top.at[d - 1], (o // S, o % S, b)))
        sends[-1].start()
    for copy in sends:
        copy.wait()
    peak[...] = jnp.max(tops[...], axis=0)


def finish(vel, par, S, B):
    _, chans, width = vel.shape
    dma = pltpu.SemaphoreType.DMA
    vmem = pl.BlockSpec(memory_space=pltpu.VMEM)
    return pl.pallas_call(
        functools.partial(tail_kernel, S, B),
        out_shape=[
            jax.ShapeDtypeStruct((2, chans, width * B // 2), jnp.float32),
            jax.ShapeDtypeStruct((8, 128), jnp.float32),
        ],
        in_specs=[vmem] * 2,
        out_specs=[vmem] * 2,
        scratch_shapes=[
            pltpu.VMEM((2, chans, width), jnp.bfloat16),
            pltpu.VMEM((B, chans, width), jnp.float32),
            pltpu.VMEM((2 * S, 8, 128), jnp.float32),
            dma((2,)), dma((2,)), dma((B - 1,)), dma((B - 1,)),
            dma((2 * S - 1,)), dma((2 * S - 1,)),
        ],
        compiler_params=pltpu.CompilerParams(collective_id=1, has_side_effects=True),
    )(vel, par)


def per_device(
    img_hidden, txt_hidden, img_mod, txt_mod, out_mod, w_qkv, w_txt_kv, w_out,
    w_fc1, w_fc2, w_proj, latent, lengths, t_index, stride, guide,
):
    seq_size, blk_size = lax.axis_size("seq"), lax.axis_size("blk")
    group = seq_size // 2
    seq_at, blk_at, half = lax.axis_index("seq"), lax.axis_index("blk"), lax.axis_index("cfg")
    prompt = seq_at // group
    img_rows = img_hidden.shape[2]
    rows = 2 * img_rows
    own_rows = rows // blk_size

    def pick(values):
        return lax.dynamic_index_in_dim(values, prompt, 0, keepdims=False)

    slots = txt_hidden.shape[2]
    padded = jnp.pad(txt_hidden[0], ((0, 0), (0, -slots % 16), (0, 0)))
    image, text = gather_tokens(img_hidden[0], padded, seq_size, blk_size)

    mod = pick(img_mod[0])
    tmod = pick(txt_mod[0])
    fmod = pick(out_mod[0])
    attn_in = modulate(image, mod[1:2], mod[0:1])
    keys = dot(attn_in, w_qkv[1]).astype(jnp.bfloat16)
    values = dot(attn_in, w_qkv[2]).astype(jnp.bfloat16)
    pieces = [(keys, values)]
    for k in range(1, group):
        turn = [
            (i, (i // group) * group + (i + k) % group) for i in range(seq_size)
        ]
        pieces.append((lax.ppermute(keys, "seq", turn), lax.ppermute(values, "seq", turn)))
    queries = dot(attn_in, w_qkv[0]).astype(jnp.bfloat16)
    text_norm = modulate(text, tmod[0:1], tmod[1:2])
    extra = -text.shape[0] % TEXT_PAD
    text_norm = jnp.pad(text_norm, ((0, extra), (0, 0)))
    text_keys = dot(text_norm, w_txt_kv[0]).astype(jnp.bfloat16)
    text_values = dot(text_norm, w_txt_kv[1]).astype(jnp.bfloat16)
    at = jnp.arange(text_norm.shape[0], dtype=jnp.int32)
    each = padded.shape[1]
    live = (at % each < slots) & (at // each * slots + at % each < pick(lengths[0]))
    live = (live & (at < text.shape[0])).astype(jnp.float32)[None]

    model_width = w_out.shape[1]
    block = jnp.concatenate([w_out, w_proj], axis=1)
    block = jnp.pad(block, ((0, 0), (0, -block.shape[1] % 128)))
    state = None
    for at, (k, v) in enumerate(pieces):
        tail = (live, text_keys, text_values) if at == len(pieces) - 1 else None
        state = attend_piece(queries, k, v, state, tail, block, seq_size, blk_size)
        if at == 0:
            *state, weights = state
    (attended,) = state
    full_out = weights[:, :model_width]
    full_proj = weights[:, model_width:model_width + w_proj.shape[1]]
    resid_one = (image.astype(jnp.float32) + mod[2:3] * dot(attended, full_out)).astype(
        jnp.bfloat16
    )
    mlp_in = modulate(resid_one, mod[4:5], mod[3:4])
    hidden_units = jax.nn.gelu(dot(mlp_in, w_fc1), approximate=True).astype(jnp.bfloat16)
    mlp_sum = lax.psum_scatter(
        dot(hidden_units, w_fc2).astype(jnp.bfloat16), "blk", scatter_dimension=0, tiled=True
    ).astype(jnp.float32)
    resid_own = lax.dynamic_slice_in_dim(resid_one, blk_at * own_rows, own_rows, 0)
    resid_two = (resid_own.astype(jnp.float32) + mod[5:6] * mlp_sum).astype(jnp.bfloat16)
    final_in = modulate(resid_two, fmod[0:1], fmod[1:2])
    velocity = lax.dot_general(
        full_proj, final_in, (((0,), (1,)), ((), ())), preferred_element_type=jnp.float32
    ).astype(jnp.bfloat16)
    velocity = velocity.reshape(2, velocity.shape[0] // 2, own_rows)
    step_size = noise_level(t_index + stride) - noise_level(t_index)
    chunk_prompt = jnp.where(blk_at < blk_size // 2, prompt, 1 - prompt)
    par = jnp.stack([guide[chunk_prompt], step_size[chunk_prompt]])
    par = jnp.broadcast_to(par[:, None], (2, own_rows))
    update, peak = finish(velocity, par, seq_size, blk_size)
    return (latent + update.transpose(0, 2, 1), peak[:2, 0])


def solution(mesh):
    placed = (
        P("cfg", None, "seq", "blk"),
        P("cfg", None, "seq", "blk"),
        P("cfg", None, None, None),
        P("cfg", None, None, None),
        P("cfg", None, None, None),
        P(None, None, "blk"),
        P(None, None, "blk"),
        P("blk", None),
        P(None, "blk"),
        P("blk", None),
        P("blk", None),
        P(None, "seq", "cfg"),
        P("cfg", None),
        P(),
        P(),
        P(),
    )
    return jax.shard_map(
        per_device,
        mesh=mesh,
        in_specs=placed,
        out_specs=(P(None, "seq", "cfg"), P()),
        check_vma=False,
    )
```

```python
import functools

import jax
import jax.numpy as jnp
from jax import lax
from jax.experimental import pallas as pl
from jax.experimental.pallas import tpu as pltpu
from jax.sharding import PartitionSpec as P

HEAD = 64
STEPS = 28
EPSILON = 1e-06
PAIR = 2 * HEAD
Q_ROWS = 256
TEXT_PAD = 256


def normalize(values):
    values = values.astype(jnp.float32)
    center = jnp.mean(values, axis=-1, keepdims=True)
    spread = jnp.mean(jnp.square(values - center), axis=-1, keepdims=True)
    return (values - center) * lax.rsqrt(spread + EPSILON)


def modulate(values, scale_row, shift_row):
    return (normalize(values) * (1.0 + scale_row) + shift_row).astype(jnp.bfloat16)


def dot(a, b):
    return jnp.dot(a, b, preferred_element_type=jnp.float32)


def noise_level(step_index):
    remain = 1.0 - step_index.astype(jnp.float32) / STEPS
    return 3.0 * remain / (1.0 + 2.0 * remain)


MESH = pl.DeviceIdType.MESH
CHUNKS = 4


def remote(src, dst, send, recv, target):
    return pltpu.make_async_remote_copy(
        src_ref=src, dst_ref=dst, send_sem=send, recv_sem=recv,
        device_id=target, device_id_type=MESH,
    )


def at_ends():
    h, i = pl.program_id(0), pl.program_id(1)
    pairs, blocks = pl.num_programs(0), pl.num_programs(1)
    return h, i, blocks, (h == 0) & (i == 0), (h == pairs - 1) & (i == blocks - 1)


def greet(targets):
    barrier = pltpu.get_barrier_semaphore()
    for target in targets:
        pl.semaphore_signal(barrier, inc=1, device_id=target, device_id_type=MESH)
    pl.semaphore_wait(barrier, len(targets))


def attend_kernel(first, last, S, B, steps, *refs):
    refs = list(refs)
    q_ref, k_ref, v_ref = refs[:3]
    refs = refs[3:]
    if not first:
        acc_in, top_in = refs[:2]
        refs = refs[2:]
    if last:
        live_ref, tk_ref, tv_ref = refs[:3]
        refs = refs[3:]
    s_at, b, c = lax.axis_index("seq"), lax.axis_index("blk"), lax.axis_index("cfg")
    h_at, i_at, blocks, opening, closing = at_ends()
    peers = [(c, s_at, (b + d) % B) for d in range(1, B)]
    if first:
        w_ref, refs = refs[0], refs[1:]
        *refs, s_w, r_w, s_x, r_x, w_sem = refs
        w_full, refs = refs[-1], refs[:-1]
        depth = w_ref.shape[0]
        half = depth // 2

        def share(d):
            rows = pl.ds(pl.multiple_of(b * depth + c * half, half), half)
            return remote(
                w_ref.at[pl.ds(pl.multiple_of(c * half, half), half)], w_full.at[rows],
                s_w.at[d - 1], r_w.at[d - 1], peers[d - 1])

        def cross(d):
            rows = pl.ds(pl.multiple_of((b + B - d) % B * depth + c * half, half), half)
            return remote(
                w_full.at[rows], w_full.at[rows], s_x.at[d - 1], r_x.at[d - 1], (1 - c, s_at, b))

        def keep():
            rows = pl.ds(pl.multiple_of(b * depth, depth), depth)
            return pltpu.make_async_copy(w_ref, w_full.at[rows], w_sem.at[0])

        @pl.when(opening)
        def _():
            greet(peers + [(1 - c, s_at, b)])
            for d in range(1, B):
                share(d).start()
            keep().start()

    if last:
        *refs, held, s_o, r_o, l_o = refs

        def place(at):
            return refs[-1].at[
                pl.ds(pl.multiple_of(at % steps[1] * Q_ROWS, Q_ROWS), Q_ROWS),
                pl.ds(pl.multiple_of(b * (steps[0] * PAIR) + at // steps[1] * PAIR, PAIR), PAIR),
            ]

        def give(at, d):
            return remote(
                held.at[at], place(at), s_o.at[d - 1, at], r_o.at[d - 1, at], peers[d - 1])

        def own_copy(at):
            return pltpu.make_async_copy(held.at[at], place(at), l_o.at[at])

        if not first:
            @pl.when(opening)
            def _():
                greet(peers)

    q = q_ref[...]
    lane = lax.broadcasted_iota(jnp.int32, (1, PAIR), 1)
    scale = HEAD ** (-0.5)
    results = []
    for h in range(2):
        own = (lane < HEAD) if h == 0 else (lane >= HEAD)
        qh = jnp.where(own, q, jnp.zeros_like(q))
        pieces = [(k_ref[...], v_ref[...], None)]
        if last:
            pieces.append((tk_ref[...], tv_ref[...], live_ref[...] > 0.5))
        scores = []
        top = None if first else top_in[h]
        for k, v, live in pieces:
            s = lax.dot_general(qh, k, (((1,), (1,)), ((), ())), preferred_element_type=jnp.float32)
            if live is not None:
                s = jnp.where(live, s, -jnp.inf)
            scores.append(s)
            peak = jnp.max(s, axis=-1, keepdims=True)
            if top is None:
                top = jnp.broadcast_to(peak, (q.shape[0], PAIR))
            else:
                top = jnp.maximum(top, peak)
        acc = None if first else acc_in[h] * jnp.exp((top_in[h] - top) * scale)
        for (k, v, live), s in zip(pieces, scores):
            p = jnp.exp((s - top[:, :1]) * scale).astype(jnp.bfloat16)
            vh = jnp.where(own, v, jnp.ones_like(v))
            part = dot(p, vh)
            acc = part if acc is None else acc + part
        results.append((acc, top))
    if last:
        outs = [acc / pltpu.roll(acc, HEAD, 1) for acc, _ in results]
        now = h_at * steps[1] + i_at
        held[now] = jnp.where(lane < HEAD, outs[0], outs[1]).astype(jnp.bfloat16)
        for d in range(1, B):
            give(now, d).start()
        own_copy(now).start()

        @pl.when(closing)
        def _():
            def drain(at, carry):
                for d in range(1, B):
                    give(at, d).wait()
                own_copy(at).wait()
                return carry

            lax.fori_loop(0, steps[0] * steps[1], drain, 0)
    else:
        acc_out, top_out = refs
        for h in range(2):
            acc_out[h] = results[h][0]
            top_out[h] = results[h][1]
    if first:
        @pl.when(closing)
        def _():
            for d in range(1, B):
                share(d).wait()
                cross(d).start()
            for d in range(1, B):
                cross(d).wait()
            keep().wait()


def attend_piece(queries, keys, values, state, text, weights, S, B):
    rows, width = queries.shape
    count = keys.shape[0]
    pairs = width // PAIR
    steps = (pairs, rows // Q_ROWS)
    total = steps[0] * steps[1]
    dma = pltpu.SemaphoreType.DMA
    first, last = state is None, text is not None
    q_spec = pl.BlockSpec((Q_ROWS, PAIR), lambda h, i: (i, h))
    kv_spec = pl.BlockSpec((count, PAIR), lambda h, i: (0, h))
    s_spec = pl.BlockSpec((2, Q_ROWS, PAIR), lambda h, i: (h, i, 0))
    anywhere = pl.BlockSpec(memory_space=pl.ANY)
    args, specs = [queries, keys, values], [q_spec, kv_spec, kv_spec]
    out_shape, out_specs, scratch = [], [], []
    if not first:
        args += list(state)
        specs += [s_spec, s_spec]
    if last:
        args += list(text)
        t_spec = pl.BlockSpec((text[1].shape[0], PAIR), lambda h, i: (0, h))
        live_spec = pl.BlockSpec(text[0].shape, lambda h, i: (0, 0))
        specs += [live_spec, t_spec, t_spec]
        out_shape += [jax.ShapeDtypeStruct((rows, B * width), jnp.bfloat16)]
        out_specs += [anywhere]
        scratch += [
            pltpu.VMEM((total, Q_ROWS, PAIR), jnp.bfloat16),
            dma((B - 1, total)), dma((B - 1, total)), dma((total,)),
        ]
    else:
        out_shape += [jax.ShapeDtypeStruct((2 * pairs, rows, PAIR), jnp.float32)] * 2
        out_specs += [s_spec, s_spec]
    if first:
        args.append(weights)
        specs.append(anywhere)
        depth, across = weights.shape
        out_shape.append(jax.ShapeDtypeStruct((B * depth, across), jnp.bfloat16))
        out_specs.append(anywhere)
        scratch += [dma((B - 1,))] * 4 + [dma((1,))]
    reach = {"collective_id": 2 if first else 3, "has_side_effects": True} if first or last else {}
    return pl.pallas_call(
        functools.partial(attend_kernel, first, last, S, B, steps),
        grid=steps,
        in_specs=specs,
        out_specs=out_specs,
        out_shape=out_shape,
        scratch_shapes=scratch,
        compiler_params=pltpu.CompilerParams(vmem_limit_bytes=40 * 1024 * 1024, **reach),
        cost_estimate=pl.CostEstimate(
            flops=8 * rows * count * width,
            bytes_accessed=8 * rows * width,
            transcendentals=rows * count * width // HEAD,
        ),
    )(*args)


def gather_kernel(S, B, img, txt, out, tout, s_own, r_own, s_swap, r_swap, s_fwd, r_fwd,
                  s_txt, r_txt, s_tf, r_tf, local):
    s, b, c = lax.axis_index("seq"), lax.axis_index("blk"), lax.axis_index("cfg")
    group = S // 2
    p = s // group
    sp = (s + group) % S
    n, w = img.shape[1:]
    tn = txt.shape[1]
    step = n // CHUNKS
    cols = pl.ds(pl.multiple_of(b * w, w), w)
    barrier = pltpu.get_barrier_semaphore()
    for d in range(1, S):
        pl.semaphore_signal(barrier, inc=1, device_id=(c, (s + d) % S, b), device_id_type=MESH)
    for d in range(1, B):
        pl.semaphore_signal(barrier, inc=1, device_id=(c, s, (b + d) % B), device_id_type=MESH)
    pl.semaphore_wait(barrier, S + B - 2)

    swaps = []
    for j in range(CHUNKS):
        swaps.append(remote(
            img.at[1 - p, pl.ds(j * step, step)], out.at[pl.ds(n + j * step, step), cols],
            s_swap.at[j], r_swap.at[j], (c, sp, b)))
        swaps[-1].start()
    texts = []
    here = pl.ds(pl.multiple_of(s * tn, tn), tn)
    for d in range(1, S):
        t = (s + d) % S
        texts.append(remote(
            txt.at[t // group], tout.at[here, cols], s_txt.at[d - 1], r_txt.at[d - 1], (c, t, b)))
        texts[-1].start()
    own = []
    for d in range(1, B):
        own.append(remote(
            img.at[p], out.at[pl.ds(0, n), cols], s_own.at[d - 1], r_own.at[d - 1],
            (c, s, (b + d) % B)))
        own[-1].start()
    keep = pltpu.make_async_copy(img.at[p], out.at[pl.ds(0, n), cols], local.at[0])
    keep.start()
    keep_text = pltpu.make_async_copy(txt.at[p], tout.at[here, cols], local.at[1])
    keep_text.start()
    keep_text.wait()
    for copy in texts:
        copy.wait()
    spread = []
    for d in range(1, B):
        spread.append(remote(
            tout.at[:, cols], tout.at[:, cols], s_tf.at[d - 1], r_tf.at[d - 1],
            (c, s, (b + d) % B)))
        spread[-1].start()
    for j in range(CHUNKS):
        swaps[j].wait()
        part = out.at[pl.ds(n + j * step, step), cols]
        for d in range(1, B):
            spread.append(remote(
                part, part, s_fwd.at[j, d - 1], r_fwd.at[j, d - 1], (c, s, (b + d) % B)))
            spread[-1].start()
    keep.wait()
    for copy in own + spread:
        copy.wait()


def gather_tokens(img, txt, S, B):
    n, w = img.shape[1:]
    tn = txt.shape[1]
    dma = pltpu.SemaphoreType.DMA
    shapes = [(B - 1,)] * 2 + [(CHUNKS,)] * 2 + [(CHUNKS, B - 1)] * 2 + [(S - 1,)] * 2 + [(B - 1,)] * 2 + [(2,)]
    return pl.pallas_call(
        functools.partial(gather_kernel, S, B),
        out_shape=[
            jax.ShapeDtypeStruct((2 * n, B * w), jnp.bfloat16),
            jax.ShapeDtypeStruct((S * tn, B * w), jnp.bfloat16),
        ],
        in_specs=[pl.BlockSpec(memory_space=pl.ANY)] * 2,
        out_specs=[pl.BlockSpec(memory_space=pl.ANY)] * 2,
        scratch_shapes=[dma(shape) for shape in shapes],
        compiler_params=pltpu.CompilerParams(collective_id=0, has_side_effects=True),
    )(img, txt)


def tail_kernel(S, B, vel, par, out, peak, inbox, box, tops, s_in, r_in, s_box, r_box, s_top, r_top):
    s, b, c = lax.axis_index("seq"), lax.axis_index("blk"), lax.axis_index("cfg")
    group, side = S // 2, B // 2
    p = s // group
    high = b // side
    t = (s + group * high) % S
    me = c * S + s
    barrier = pltpu.get_barrier_semaphore()
    for d in range(1, 2 * S):
        o = (me + d) % (2 * S)
        pl.semaphore_signal(barrier, inc=1, device_id=(o // S, o % S, b), device_id_type=MESH)
    for d in range(1, B):
        pl.semaphore_signal(barrier, inc=1, device_id=(c, s, (b + d) % B), device_id_type=MESH)
    pl.semaphore_wait(barrier, 2 * S - 1 + B - 1)

    across = remote(vel.at[1 - c], inbox.at[c], s_in.at[0], r_in.at[0], (1 - c, t, b))
    across.start()

    @pl.when(high == 0)
    def _():
        inbox[c] = vel[c]

    @pl.when(high == 1)
    def _():
        same = remote(vel.at[c], inbox.at[c], s_in.at[1], r_in.at[1], (c, (s + group) % S, b))
        same.start()
        same.wait()

    across.wait()
    cond = inbox[0].astype(jnp.float32)
    uncond = inbox[1].astype(jnp.float32)
    box[b] = par[1:2] * (uncond + par[0:1] * (cond - uncond))
    sends = []
    for d in range(1, B):
        sends.append(remote(
            box.at[b], box.at[b], s_box.at[d - 1], r_box.at[d - 1], (c, s, (b + d) % B)))
        sends[-1].start()
    for copy in sends:
        copy.wait()
    tall = []
    width = box.shape[2]
    for k in range(2):
        which = p if k == 0 else 1 - p
        top = None
        for j in range(side):
            part = box[k * side + j]
            out[which, :, j * width:(j + 1) * width] = part
            value = jnp.max(jnp.abs(part), axis=(0, 1), keepdims=True)
            top = value if top is None else jnp.maximum(top, value)
        tall.append(top)
    row = lax.broadcasted_iota(jnp.int32, (8, 128), 0)
    tops[me] = jnp.where(row == p, tall[0], tall[1])
    sends = []
    for d in range(1, 2 * S):
        o = (me + d) % (2 * S)
        sends.append(remote(
            tops.at[me], tops.at[me], s_top.at[d - 1], r_top.at[d - 1], (o // S, o % S, b)))
        sends[-1].start()
    for copy in sends:
        copy.wait()
    peak[...] = jnp.max(tops[...], axis=0)


def finish(vel, par, S, B):
    _, chans, width = vel.shape
    dma = pltpu.SemaphoreType.DMA
    vmem = pl.BlockSpec(memory_space=pltpu.VMEM)
    return pl.pallas_call(
        functools.partial(tail_kernel, S, B),
        out_shape=[
            jax.ShapeDtypeStruct((2, chans, width * B // 2), jnp.float32),
            jax.ShapeDtypeStruct((8, 128), jnp.float32),
        ],
        in_specs=[vmem] * 2,
        out_specs=[vmem] * 2,
        scratch_shapes=[
            pltpu.VMEM((2, chans, width), jnp.bfloat16),
            pltpu.VMEM((B, chans, width), jnp.float32),
            pltpu.VMEM((2 * S, 8, 128), jnp.float32),
            dma((2,)), dma((2,)), dma((B - 1,)), dma((B - 1,)),
            dma((2 * S - 1,)), dma((2 * S - 1,)),
        ],
        compiler_params=pltpu.CompilerParams(collective_id=1, has_side_effects=True),
    )(vel, par)


def feed_kernel(B, x, w1, w2, out, held, inbox, s_sem, r_sem):
    s, b, c = lax.axis_index("seq"), lax.axis_index("blk"), lax.axis_index("cfg")
    k = pl.program_id(0)
    target = (b + 1 + k) % B
    n = out.shape[0]

    def give(at):
        return remote(
            held.at[at], inbox.at[at], s_sem.at[at], r_sem.at[at], (c, s, (b + 1 + at) % B))

    @pl.when(k == 0)
    def _():
        greet([(c, s, (b + d) % B) for d in range(1, B)])

    rows = x[pl.ds(pl.multiple_of(target * n, n), n), :]
    hidden = jax.nn.gelu(dot(rows, w1[...]), approximate=True).astype(jnp.bfloat16)
    part = dot(hidden, w2[...])

    @pl.when(k < B - 1)
    def _():
        held[k] = part.astype(jnp.bfloat16)
        give(k).start()

    @pl.when(k == B - 1)
    def _():
        total = part
        for at in range(B - 1):
            give(at).wait()
            total = total + inbox[at].astype(jnp.float32)
        out[...] = total


def feed_forward(x, w1, w2, B):
    n, width = x.shape[0] // B, w2.shape[1]
    dma = pltpu.SemaphoreType.DMA
    vmem = pl.BlockSpec(memory_space=pltpu.VMEM)
    return pl.pallas_call(
        functools.partial(feed_kernel, B),
        grid=(B,),
        out_shape=jax.ShapeDtypeStruct((n, width), jnp.float32),
        in_specs=[vmem] * 3,
        out_specs=vmem,
        scratch_shapes=[
            pltpu.VMEM((B - 1, n, width), jnp.bfloat16),
            pltpu.VMEM((B - 1, n, width), jnp.bfloat16),
            dma((B - 1,)), dma((B - 1,)),
        ],
        compiler_params=pltpu.CompilerParams(
            collective_id=4, has_side_effects=True, vmem_limit_bytes=44 * 1024 * 1024
        ),
    )(x, w1, w2)


def per_device(
    img_hidden, txt_hidden, img_mod, txt_mod, out_mod, w_qkv, w_txt_kv, w_out,
    w_fc1, w_fc2, w_proj, latent, lengths, t_index, stride, guide,
):
    seq_size, blk_size = lax.axis_size("seq"), lax.axis_size("blk")
    group = seq_size // 2
    seq_at, blk_at, half = lax.axis_index("seq"), lax.axis_index("blk"), lax.axis_index("cfg")
    prompt = seq_at // group
    img_rows = img_hidden.shape[2]
    rows = 2 * img_rows
    own_rows = rows // blk_size

    def pick(values):
        return lax.dynamic_index_in_dim(values, prompt, 0, keepdims=False)

    slots = txt_hidden.shape[2]
    padded = jnp.pad(txt_hidden[0], ((0, 0), (0, -slots % 16), (0, 0)))
    image, text = gather_tokens(img_hidden[0], padded, seq_size, blk_size)

    mod = pick(img_mod[0])
    tmod = pick(txt_mod[0])
    fmod = pick(out_mod[0])
    attn_in = modulate(image, mod[1:2], mod[0:1])
    keys = dot(attn_in, w_qkv[1]).astype(jnp.bfloat16)
    values = dot(attn_in, w_qkv[2]).astype(jnp.bfloat16)
    pieces = [(keys, values)]
    for k in range(1, group):
        turn = [
            (i, (i // group) * group + (i + k) % group) for i in range(seq_size)
        ]
        pieces.append((lax.ppermute(keys, "seq", turn), lax.ppermute(values, "seq", turn)))
    queries = dot(attn_in, w_qkv[0]).astype(jnp.bfloat16)
    text_norm = modulate(text, tmod[0:1], tmod[1:2])
    extra = -text.shape[0] % TEXT_PAD
    text_norm = jnp.pad(text_norm, ((0, extra), (0, 0)))
    text_keys = dot(text_norm, w_txt_kv[0]).astype(jnp.bfloat16)
    text_values = dot(text_norm, w_txt_kv[1]).astype(jnp.bfloat16)
    at = jnp.arange(text_norm.shape[0], dtype=jnp.int32)
    each = padded.shape[1]
    live = (at % each < slots) & (at // each * slots + at % each < pick(lengths[0]))
    live = (live & (at < text.shape[0])).astype(jnp.float32)[None]

    model_width = w_out.shape[1]
    block = jnp.concatenate([w_out, w_proj], axis=1)
    block = jnp.pad(block, ((0, 0), (0, -block.shape[1] % 128)))
    state = None
    for at, (k, v) in enumerate(pieces):
        tail = (live, text_keys, text_values) if at == len(pieces) - 1 else None
        state = attend_piece(queries, k, v, state, tail, block, seq_size, blk_size)
        if at == 0:
            *state, weights = state
    (attended,) = state
    full_out = weights[:, :model_width]
    full_proj = weights[:, model_width:model_width + w_proj.shape[1]]
    resid_one = (image.astype(jnp.float32) + mod[2:3] * dot(attended, full_out)).astype(
        jnp.bfloat16
    )
    mlp_in = modulate(resid_one, mod[4:5], mod[3:4])
    mlp_sum = feed_forward(mlp_in, w_fc1, w_fc2, blk_size)
    resid_own = lax.dynamic_slice_in_dim(resid_one, blk_at * own_rows, own_rows, 0)
    resid_two = (resid_own.astype(jnp.float32) + mod[5:6] * mlp_sum).astype(jnp.bfloat16)
    final_in = modulate(resid_two, fmod[0:1], fmod[1:2])
    velocity = lax.dot_general(
        full_proj, final_in, (((0,), (1,)), ((), ())), preferred_element_type=jnp.float32
    ).astype(jnp.bfloat16)
    velocity = velocity.reshape(2, velocity.shape[0] // 2, own_rows)
    step_size = noise_level(t_index + stride) - noise_level(t_index)
    chunk_prompt = jnp.where(blk_at < blk_size // 2, prompt, 1 - prompt)
    par = jnp.stack([guide[chunk_prompt], step_size[chunk_prompt]])
    par = jnp.broadcast_to(par[:, None], (2, own_rows))
    update, peak = finish(velocity, par, seq_size, blk_size)
    return (latent + update.transpose(0, 2, 1), peak[:2, 0])


def solution(mesh):
    placed = (
        P("cfg", None, "seq", "blk"),
        P("cfg", None, "seq", "blk"),
        P("cfg", None, None, None),
        P("cfg", None, None, None),
        P("cfg", None, None, None),
        P(None, None, "blk"),
        P(None, None, "blk"),
        P("blk", None),
        P(None, "blk"),
        P("blk", None),
        P("blk", None),
        P(None, "seq", "cfg"),
        P("cfg", None),
        P(),
        P(),
        P(),
    )
    return jax.shard_map(
        per_device,
        mesh=mesh,
        in_specs=placed,
        out_specs=(P(None, "seq", "cfg"), P()),
        check_vma=False,
    )
```
